256 devices in a mesh: chan: 128 (over x, z, y), blk: 2 (over core).
Axes of the slice: x: 4, y: 4, z: 8, core: 2. Of those that a mesh axis runs over, the one named last changes fastest.
Arguments:
- generator: bfloat16 [128, 1536, 1536], P('chan', 'blk'), may hold values from -6 to 6
- hamiltonian: bfloat16 [128, 1536, 1536], P('chan', 'blk'), may hold values from -0.15625 to 0.15625
- pp_occupancy: float32 [128, 1536], P('chan'), may hold values from -1 to 1
- ph_occupancy: float32 [128, 1536], P('chan'), may hold values from -1 to 1
- lengths: int32 [128], P('chan'), may hold values from 384 to 1536, as said below
- partner: int32 [128, 128], P('chan'), may hold values from 0 to 127, each once within a row
- coupling: float32 [128, 128], P('chan'), may hold values from 0.5 to 2
- degeneracy: float32 [128], P('chan'), may hold values from 1 to 30
- orbital: int32 [128, 1536], P('chan', 'blk'), may hold values from 0 to 239
Outputs:
- two_body: bfloat16 [128, 1536, 1536], P('chan', 'blk')
- one_body: float32 [240], replicated
The draws below stay inside these ranges and needn't reach their ends.
Inputs may be any that keep to these rules, and one draw needn't show every extreme that they name: `lengths`: some channel has the full length 1536.
All inputs are finite; a program needn't handle non-finite values.
Results may differ from the reference program's by a relative error of at most 0.007.
Values may be sent and summed in bfloat16 or wider, within the bound.
No kernel may reach another device: no remote copies, remote signals or barrier semaphores. Data moves between devices by JAX's collectives and lax.ppermute only.
A program may use at most 128 MiB of HBM per device.

```python
import math
import jax
import jax.numpy as jnp
from jax import lax

M = 1536
NOB = 240
NCH = 128
PIECE = 6
N_CHAN = 128
N_BLK = 2


def draw_lengths(key, part):
    first_key, second_key = jax.random.split(jax.random.fold_in(key, 11))
    sizes = jax.random.randint(first_key, (NCH,), M // 4, M + 1, dtype=jnp.int32)
    chosen = jax.random.randint(second_key, (), 0, NCH, dtype=jnp.int32)
    return jnp.where(jnp.arange(NCH, dtype=jnp.int32) == chosen, M, sizes).astype(jnp.int32)


def touch_ends(entries, rng, least, largest):
    dims = entries.shape
    spot = [jax.random.randint(jax.random.fold_in(rng, axis), (), 0, dims[axis]) for axis in range(len(dims))]
    entries = entries.at[tuple(spot)].set(least)
    longest = dims.index(max(dims))
    spot[longest] = (spot[longest] + 1) % dims[longest]
    return entries.at[tuple(spot)].set(largest)


def steps_of(rng, shape, cuts, smallest, top_value):
    factor_of = 1.0
    for position, blocks in cuts:
        draws = jax.random.uniform(jax.random.fold_in(jax.random.fold_in(rng, 6), position), (blocks,), jnp.float32, smallest / len(cuts), top_value / len(cuts))
        factor_of = factor_of * jnp.repeat(jnp.exp(draws), shape[position] // blocks).reshape((-1,) + (1,) * (len(shape) - 1 - position))
    return factor_of


def bell_draw(key, shape, deviation, most, cuts=(), kind=jnp.bfloat16):
    entries = deviation * jax.random.normal(key, shape, jnp.float32)
    if cuts:
        entries = entries * steps_of(key, shape, cuts, -0.22, 0.18)
    return jnp.clip(entries, -most, most).astype(kind)


def setup_inputs(seed: int = 0) -> dict:
    seeds = jax.random.split(jax.random.key(seed), 10)
    return {
        "generator": bell_draw(seeds[0], (NCH, M, M), 1.0, 6.0, ((0, 128), (1, 2))),
        "hamiltonian": bell_draw(seeds[1], (NCH, M, M), M ** -0.5, 0.15625, ((0, 128), (1, 2))),
        "pp_occupancy": jnp.clip(jax.random.uniform(seeds[2], (NCH, M), jnp.float32, -1.0, 1.0) * steps_of(seeds[2], (NCH, M), ((0, 128),), -0.4, 0.0), -1.0, 1.0),
        "ph_occupancy": jnp.clip(jax.random.uniform(seeds[3], (NCH, M), jnp.float32, -1.0, 1.0) * steps_of(seeds[3], (NCH, M), ((0, 128),), -0.4, 0.0), -1.0, 1.0),
        "lengths": draw_lengths(jax.random.fold_in(seeds[9], 71), 0),
        "partner": jax.vmap(lambda own: jax.random.permutation(own, N_CHAN))(jax.random.split(seeds[5], NCH)).reshape((NCH, N_CHAN)).astype(jnp.int32),
        "coupling": jnp.clip(jnp.exp(math.log(2.0) - 1.3862944 * jax.random.uniform(seeds[6], (NCH, N_CHAN), jnp.float32) ** steps_of(seeds[6], (NCH, N_CHAN), ((0, 128),), -0.2, 0.2)), 0.5, 2.0),
        "degeneracy": jnp.clip(jnp.exp(math.log(30.0) - 3.4011974 * jax.random.uniform(seeds[7], (NCH,), jnp.float32) ** steps_of(seeds[7], (NCH,), ((0, 128),), -0.2, 0.2)), 1.0, 30.0),
        "orbital": touch_ends(jax.random.randint(seeds[8], (NCH, M), 0, NOB), jax.random.fold_in(seeds[8], 1), 0, NOB - 1).astype(jnp.int32),
    }


def commute(first_mat, second_mat, occupancy):
    left = (first_mat.astype(jnp.float32) * occupancy[None, :]).astype(jnp.bfloat16)
    right = (second_mat.astype(jnp.float32) * occupancy[None, :]).astype(jnp.bfloat16)
    return jnp.dot(left, second_mat, preferred_element_type=jnp.float32) - jnp.dot(right, first_mat, preferred_element_type=jnp.float32)

def commute_items(items):
    return commute(items[0], items[1], items[2])

def recouple(matrices, partner, coupling):
    layout = (NCH, N_BLK, N_CHAN, PIECE, M)
    pieces = matrices.reshape(layout)
    scaled = (pieces.astype(jnp.float32) * coupling[:, None, :, None, None]).astype(jnp.bfloat16)
    sender_slot = jnp.argsort(partner, axis=1).astype(jnp.int32)
    moved = jnp.take_along_axis(scaled, sender_slot[:, None, :, None, None], axis=2)
    return jnp.transpose(moved, (2, 1, 0, 3, 4)).reshape(NCH, M, M)

def reference(generator, hamiltonian, pp_occupancy, ph_occupancy, lengths, partner, coupling, degeneracy, orbital):
    positions = jnp.arange(M, dtype=jnp.int32)
    live_cols = positions[None, :] < lengths[:, None]
    live_mask = live_cols[:, :, None] & live_cols[:, None, :]
    gen_live = jnp.where(live_mask, generator, jnp.zeros((), generator.dtype))
    ham_live = jnp.where(live_mask, hamiltonian, jnp.zeros((), hamiltonian.dtype))
    ladder = lax.map(commute_items, (gen_live, ham_live, pp_occupancy))
    gen_cross = recouple(gen_live, partner, coupling)
    ham_cross = recouple(ham_live, partner, coupling)
    crossed = lax.map(commute_items, (gen_cross, ham_cross, ph_occupancy)).astype(jnp.bfloat16)
    layout = (NCH, N_BLK, N_CHAN, PIECE, M)
    turned = jnp.transpose(crossed.reshape(layout), (2, 1, 0, 3, 4))
    fetched = jnp.take_along_axis(turned, partner.astype(jnp.int32)[:, None, :, None, None], axis=2)
    restored = (fetched.astype(jnp.float32) * coupling[:, None, :, None, None]).reshape(NCH, M, M)
    combined = jnp.where(live_mask, ladder + restored, jnp.zeros((), jnp.float32))
    two_body = combined.astype(jnp.bfloat16)
    diagonal = jnp.diagonal(combined, axis1=1, axis2=2) * degeneracy[:, None]
    summed = jax.ops.segment_sum(diagonal.reshape(-1), orbital.reshape(-1).astype(jnp.int32), num_segments=NOB)
    one_body = summed / (8.0 * math.sqrt(NCH * M / NOB))
    return (two_body, one_body)
```

```python
import math

import jax
import jax.numpy as jnp
from jax import lax
from jax.experimental import pallas as pl
from jax.experimental.pallas import tpu as pltpu
from jax.sharding import Mesh
from jax.sharding import PartitionSpec as P

NOB = 240
CHAN = ("chan_0", "chan_1", "chan_2")
SIZES = (("blk", 2), ("chan_0", 4), ("chan_2", 4), ("chan_1", 8))
M = 1536
ROWS = 768
NCH = 128
Q = 6
WIDE = 1152
TAIL = 384
GROUP = 8
GROUP_ROWS = GROUP * Q
F32 = jnp.float32
BF16 = jnp.bfloat16


def put_packed(dst, at, src, row, scale=None):
    def part(rows, columns):
        block = src[rows, columns]
        return block if scale is None else block * scale

    dst[at : at + Q, :] = part(slice(row, row + Q), slice(0, WIDE))
    for t in range(3):
        dst[at + Q : at + Q + 2, t * TAIL : (t + 1) * TAIL] = part(
            slice(row + 2 * t, row + 2 * t + 2), slice(WIDE, M)
        )


def put_unpacked(dst, row, message):
    dst[row : row + Q, 0:WIDE] = message[0:Q]
    for t in range(3):
        dst[row + 2 * t : row + 2 * t + 2, WIDE:M] = message[Q : Q + 2, t * TAIL : (t + 1) * TAIL]


def live_block(blk, step, length):
    rows = blk * ROWS + step * GROUP_ROWS + lax.broadcasted_iota(jnp.int32, (GROUP_ROWS, M), 0)
    columns = lax.broadcasted_iota(jnp.int32, (GROUP_ROWS, M), 1)
    return (rows < length) & (columns < length)


def pack_kernel(ints, partner, coupling, gen, ham, out, stage_gen, stage_ham, message):
    step = pl.program_id(0)
    live = live_block(ints[0], step, ints[1])
    stage_gen[...] = jnp.where(live, gen[...].astype(F32), 0.0)
    stage_ham[...] = jnp.where(live, ham[...].astype(F32), 0.0)
    for j in range(GROUP):
        piece = step * GROUP + j
        scale = coupling[piece]
        put_packed(message.at[j % 2], 0, stage_gen, j * Q, scale)
        put_packed(message.at[j % 2], 8, stage_ham, j * Q, scale)
        out[partner[piece]] = message[j % 2].astype(BF16)


def pack(ints, partner, coupling, generator, hamiltonian):
    smem = pl.BlockSpec(memory_space=pltpu.SMEM)
    block = pl.BlockSpec((GROUP_ROWS, M), lambda i: (i, 0))
    return pl.pallas_call(
        pack_kernel,
        out_shape=jax.ShapeDtypeStruct((NCH, 16, WIDE), BF16),
        grid=(NCH // GROUP,),
        in_specs=[smem, smem, smem, block, block],
        out_specs=pl.BlockSpec((NCH, 16, WIDE), lambda i: (0, 0, 0)),
        scratch_shapes=[
            pltpu.VMEM((GROUP_ROWS, M), F32),
            pltpu.VMEM((GROUP_ROWS, M), F32),
            pltpu.VMEM((2, 16, WIDE), F32),
        ],
        compiler_params=pltpu.CompilerParams(vmem_limit_bytes=32 * 2**20),
        cost_estimate=pl.CostEstimate(flops=10**7, bytes_accessed=4 * ROWS * M * 2, transcendentals=0),
    )(ints, partner, coupling, generator, hamiltonian)


CHUNK = 192
CHUNK_PIECES = CHUNK // Q


def cross_kernel(ints, occupancy, own, other, out, right, stage_gen, stage_ham, product, message):
    blk = ints[0]

    def unpack(source, at):
        @pl.loop(0, NCH // GROUP)
        def _(g):
            for j in range(GROUP):
                both = source[g * GROUP + j].astype(F32)
                put_unpacked(stage_gen, j * Q, both[0:8])
                put_unpacked(stage_ham, j * Q, both[8:16])
            row = pl.multiple_of(at + g * GROUP_ROWS, 16)
            right[pl.ds(row, GROUP_ROWS), :] = stage_ham[...].astype(BF16)
            right[pl.ds(row + M, GROUP_ROWS), :] = stage_gen[...].astype(BF16)

    unpack(own, blk * ROWS)
    unpack(other, (1 - blk) * ROWS)

    @pl.loop(0, ROWS // CHUNK)
    def _(c):
        row = pl.multiple_of(blk * ROWS + c * CHUNK, 16)
        occ = occupancy[...]
        gen_left = (right[pl.ds(row + M, CHUNK), :].astype(F32) * occ).astype(BF16)
        ham_left = (right[pl.ds(row, CHUNK), :].astype(F32) * -occ).astype(BF16)
        left = jnp.concatenate([gen_left, ham_left], axis=1)
        product[...] = (
            jnp.dot(left, right[...], preferred_element_type=F32).astype(BF16).astype(F32)
        )
        for j in range(CHUNK_PIECES // 2):
            put_packed(message.at[j % 2], 0, product, 2 * j * Q)
            put_packed(message.at[j % 2], 8, product, (2 * j + 1) * Q)
            out[c * (CHUNK_PIECES // 2) + j] = message[j % 2].astype(BF16)


def cross(ints, occupancy, own, other):
    vmem = pl.BlockSpec(memory_space=pltpu.VMEM)
    return pl.pallas_call(
        cross_kernel,
        out_shape=jax.ShapeDtypeStruct((NCH // 2, 16, WIDE), BF16),
        in_specs=[pl.BlockSpec(memory_space=pltpu.SMEM), vmem, vmem, vmem],
        out_specs=vmem,
        scratch_shapes=[
            pltpu.VMEM((2 * M, M), BF16),
            pltpu.VMEM((GROUP_ROWS, M), F32),
            pltpu.VMEM((GROUP_ROWS, M), F32),
            pltpu.VMEM((CHUNK, M), F32),
            pltpu.VMEM((2, 16, WIDE), F32),
        ],
        compiler_params=pltpu.CompilerParams(vmem_limit_bytes=44 * 2**20),
        cost_estimate=pl.CostEstimate(
            flops=4 * ROWS * M * M, bytes_accessed=10 * ROWS * M, transcendentals=0
        ),
    )(ints, occupancy, own, other)


def finish_kernel(ints, partner, coupling, back, ladder, out, diagonal, stage):
    step = pl.program_id(0)
    for j in range(GROUP):
        piece = step * GROUP + j
        source = partner[piece]
        pair = back[source // 2].astype(F32)
        message = jnp.where(source % 2 == 1, pair[8:16], pair[0:8]) * coupling[piece]
        put_unpacked(stage, j * Q, message)
    live = live_block(ints[0], step, ints[1])
    combined = jnp.where(live, ladder[...] + stage[...], 0.0)
    out[...] = combined.astype(BF16)
    rows = ints[0] * ROWS + step * GROUP_ROWS + lax.broadcasted_iota(jnp.int32, (GROUP_ROWS, M), 0)
    columns = lax.broadcasted_iota(jnp.int32, (GROUP_ROWS, M), 1)
    part = jnp.sum(jnp.where(rows == columns, combined, 0.0), axis=0, keepdims=True)

    @pl.when(step == 0)
    def _():
        diagonal[...] = part

    @pl.when(step > 0)
    def _():
        diagonal[...] += part


def finish(ints, partner, coupling, back, ladder):
    smem = pl.BlockSpec(memory_space=pltpu.SMEM)
    block = pl.BlockSpec((GROUP_ROWS, M), lambda i: (i, 0))
    return pl.pallas_call(
        finish_kernel,
        out_shape=(
            jax.ShapeDtypeStruct((ROWS, M), BF16),
            jax.ShapeDtypeStruct((1, M), F32),
        ),
        grid=(NCH // GROUP,),
        in_specs=[
            smem,
            smem,
            smem,
            pl.BlockSpec((NCH // 2, 16, WIDE), lambda i: (0, 0, 0)),
            block,
        ],
        out_specs=(block, pl.BlockSpec((1, M), lambda i: (0, 0))),
        scratch_shapes=[pltpu.VMEM((GROUP_ROWS, M), F32)],
        compiler_params=pltpu.CompilerParams(vmem_limit_bytes=32 * 2**20),
        cost_estimate=pl.CostEstimate(flops=10**7, bytes_accessed=8 * ROWS * M, transcendentals=0),
    )(ints, partner, coupling, back, ladder)


def total(values):
    for axis, size in SIZES:
        parts = [values] + [
            lax.ppermute(values, axis, [(i, i ^ d) for i in range(size)]) for d in range(1, size)
        ]
        while len(parts) > 1:
            parts = [parts[i] + parts[i + 1] for i in range(0, len(parts), 2)]
        values = parts[0]
    return values


def on_device(
    generator,
    hamiltonian,
    pp_occupancy,
    ph_occupancy,
    lengths,
    partner,
    coupling,
    degeneracy,
    orbital,
):
    blk = lax.axis_index("blk")
    ints = jnp.stack([blk.astype(jnp.int32), lengths[0]])
    gen, ham = generator[0], hamiltonian[0]
    sent = pack(ints, partner[0], coupling[0], gen, ham)
    received = lax.all_to_all(sent, CHAN, split_axis=0, concat_axis=0, tiled=True)

    live_states = jnp.arange(M, dtype=jnp.int32) < lengths[0]
    occupancy = jnp.where(live_states, pp_occupancy[0], 0.0)
    gen_all = lax.all_gather(gen, "blk", axis=0, tiled=True)
    ham_all = lax.all_gather(ham, "blk", axis=0, tiled=True)
    ladder = jnp.dot(
        (gen.astype(F32) * occupancy[None]).astype(BF16), ham_all, preferred_element_type=F32
    ) - jnp.dot((ham.astype(F32) * occupancy[None]).astype(BF16), gen_all, preferred_element_type=F32)

    other = lax.ppermute(received, "blk", [(0, 1), (1, 0)])
    crossed = cross(ints, ph_occupancy, received, other)
    returned = lax.all_to_all(
        crossed.reshape(NCH, 8, WIDE), CHAN, split_axis=0, concat_axis=0, tiled=True
    ).reshape(NCH // 2, 16, WIDE)
    two_body, diagonal = finish(ints, partner[0], coupling[0], returned, ladder)
    own = lax.dynamic_slice_in_dim(diagonal[0], blk * ROWS, ROWS, 0) * degeneracy[0]
    match = orbital[0][:, None] == jnp.arange(NOB, dtype=jnp.int32)[None, :]
    sums = jnp.sum(jnp.where(match, own[:, None], 0.0), axis=0)
    one_body = total(sums) / (8.0 * math.sqrt(NCH * M / NOB))
    return (two_body[None], one_body)


def solution(mesh):
    torus = Mesh(
        mesh.devices.reshape(4, 8, 4, mesh.shape["blk"]), ("chan_0", "chan_1", "chan_2", "blk")
    )
    in_specs = (
        P(CHAN, "blk", None),
        P(CHAN, "blk", None),
        P(CHAN, None),
        P(CHAN, None),
        P(CHAN),
        P(CHAN, None),
        P(CHAN, None),
        P(CHAN),
        P(CHAN, "blk"),
    )
    out_specs = (P(CHAN, "blk", None), P())
    return jax.shard_map(
        on_device, mesh=torus, in_specs=in_specs, out_specs=out_specs, check_vma=False
    )
```

```python
import math

import jax
import jax.numpy as jnp
from jax import lax
from jax.experimental import pallas as pl
from jax.experimental.pallas import tpu as pltpu
from jax.sharding import Mesh
from jax.sharding import PartitionSpec as P

NOB = 240
CHAN = ("chan_0", "chan_1", "chan_2")
SIZES = (("blk", 2), ("chan_0", 4), ("chan_2", 4), ("chan_1", 8))
M = 1536
ROWS = 768
NCH = 128
Q = 6
WIDE = 1152
TILES = 9
LANES = 128
SENT = 8 * (2 * TILES + 1)
TAIL = 384
GROUP = 8
GROUP_ROWS = GROUP * Q
F32 = jnp.float32
BF16 = jnp.bfloat16


VMEM_LIMIT = 62 * 2**20
STEP_ROWS = 192
STEP_GROUPS = STEP_ROWS // GROUP_ROWS
STEPS = ROWS // STEP_ROWS


def put_packed(dst, at, src, row, scale=None):
    def part(rows, columns):
        block = src[rows, columns]
        return block if scale is None else block * scale

    dst[at : at + Q, :] = part(slice(row, row + Q), slice(0, WIDE))
    for t in range(3):
        dst[at + Q : at + Q + 2, t * TAIL : (t + 1) * TAIL] = part(
            slice(row + 2 * t, row + 2 * t + 2), slice(WIDE, M)
        )


def put_unpacked(dst, row, message):
    dst[row : row + Q, 0:WIDE] = message[0:Q]
    for t in range(3):
        dst[row + 2 * t : row + 2 * t + 2, WIDE:M] = message[Q : Q + 2, t * TAIL : (t + 1) * TAIL]


def params(limit=VMEM_LIMIT):
    return pltpu.CompilerParams(vmem_limit_bytes=limit)


def cost(flops, moved):
    return pl.CostEstimate(flops=flops, bytes_accessed=moved, transcendentals=0)


def smem():
    return pl.BlockSpec(memory_space=pltpu.SMEM)


def live_block(blk, row, length):
    rows = blk * ROWS + row + lax.broadcasted_iota(jnp.int32, (GROUP_ROWS, M), 0)
    columns = lax.broadcasted_iota(jnp.int32, (GROUP_ROWS, M), 1)
    return (rows < length) & (columns < length)


def put_tiles(dst, tile, src, row, scale):
    for t in range(TILES):
        at = 8 * (tile + t)
        dst[at : at + Q, :] = src[row : row + Q, t * LANES : (t + 1) * LANES] * scale
        pair, third = row + 2 * (t // 3), WIDE + (t % 3) * LANES
        dst[at + Q : at + 8, :] = src[pair : pair + 2, third : third + LANES] * scale


def put_from_tiles(dst, row, message, tile):
    for t in range(TILES):
        at = 8 * (tile + t)
        dst[row : row + Q, t * LANES : (t + 1) * LANES] = message[at : at + Q]
        pair, third = row + 2 * (t // 3), WIDE + (t % 3) * LANES
        dst[pair : pair + 2, third : third + LANES] = message[at + Q : at + 8]


def pack_kernel(
    ints,
    partner,
    coupling,
    degeneracy,
    orbital,
    gen,
    ham,
    out,
    notes,
    stage_gen,
    stage_ham,
    stage_notes,
    message,
    ready,
    sem,
):
    step = pl.program_id(0)
    length = ints[1]

    def copy(piece):
        return pltpu.make_async_copy(ready.at[piece], out.at[partner[piece]], sem.at[piece])

    def iota(shape, dim):
        return lax.broadcasted_iota(jnp.int32, shape, dim)

    @pl.loop(0, STEP_GROUPS)
    def _(g):
        group = step * STEP_GROUPS + g
        rows = pl.ds(pl.multiple_of(g * GROUP_ROWS, 16), GROUP_ROWS)
        live = live_block(ints[0], group * GROUP_ROWS, length)
        stage_gen[...] = jnp.where(live, gen[rows, :].astype(F32), 0.0)
        stage_ham[...] = jnp.where(live, ham[rows, :].astype(F32), 0.0)

        lanes = iota((Q, LANES), 1)
        for j in range(GROUP):
            piece = group * GROUP + j
            marks = jnp.where(lanes == 4, piece, iota((Q, LANES), 0)).astype(F32)
            stage_notes[j * Q : (j + 1) * Q, :] = jnp.where(
                lanes < 4, coupling[piece] * degeneracy[0], jnp.where(lanes < 6, marks, 0.0)
            )
        here = group * GROUP_ROWS + iota((GROUP_ROWS, ROWS), 0)
        orbit = jnp.sum(
            jnp.where(iota((GROUP_ROWS, ROWS), 1) == here, orbital[...], 0.0), axis=1, keepdims=True
        )
        state = ints[0] * ROWS + group * GROUP_ROWS + iota((GROUP_ROWS, LANES), 0)
        lanes = iota((GROUP_ROWS, LANES), 1)
        filled = stage_notes[...]
        weight = jnp.where(state < length, filled, 0.0)
        high = weight.astype(BF16).astype(F32)
        middle = (weight - high).astype(BF16).astype(F32)
        low = weight - high - middle
        noted = jnp.where(lanes == 0, high, jnp.where(lanes == 1, middle, low))
        noted = jnp.where(lanes == 3, orbit, jnp.where(lanes < 3, noted, filled))
        stage_notes[...] = noted
        notes[rows, :] = noted

        for j in range(GROUP):
            piece = group * GROUP + j
            put_tiles(message.at[j], 0, stage_gen, j * Q, coupling[piece])
            put_tiles(message.at[j], TILES, stage_ham, j * Q, coupling[piece])
            message[j, SENT - 8 : SENT - 2, :] = stage_notes[j * Q : (j + 1) * Q, :]
            ready[piece] = message[j].astype(BF16)
        for j in range(GROUP):
            copy(group * GROUP + j).start()

    @pl.when(step == STEPS - 1)
    def _():
        @pl.loop(0, NCH)
        def _(piece):
            copy(piece).wait()


def pack(ints, partner, coupling, degeneracy, orbital, generator, hamiltonian):
    block = pl.BlockSpec((STEP_ROWS, M), lambda i: (i, 0))
    return pl.pallas_call(
        pack_kernel,
        out_shape=(
            jax.ShapeDtypeStruct((NCH, SENT, LANES), BF16),
            jax.ShapeDtypeStruct((ROWS, LANES), F32),
        ),
        grid=(STEPS,),
        in_specs=[
            smem(),
            smem(),
            smem(),
            smem(),
            pl.BlockSpec((1, ROWS), lambda i: (0, 0)),
            block,
            block,
        ],
        out_specs=(
            pl.BlockSpec(memory_space=pl.ANY),
            pl.BlockSpec((STEP_ROWS, LANES), lambda i: (i, 0)),
        ),
        scratch_shapes=[
            pltpu.VMEM((GROUP_ROWS, M), F32),
            pltpu.VMEM((GROUP_ROWS, M), F32),
            pltpu.VMEM((GROUP_ROWS, LANES), F32),
            pltpu.VMEM((GROUP, SENT, LANES), F32),
            pltpu.VMEM((NCH, SENT, LANES), BF16),
            pltpu.SemaphoreType.DMA((NCH,)),
        ],
        compiler_params=params(),
        cost_estimate=cost(10**7, 8 * ROWS * M),
    )(ints, partner, coupling, degeneracy, orbital, generator, hamiltonian)


def unpack_into(source, right, stage_gen, stage_ham, notes=None):
    @pl.loop(0, NCH // GROUP)
    def _(g):
        row = pl.multiple_of(g * GROUP_ROWS, 16)
        for j in range(GROUP):
            message = source[g * GROUP + j].astype(F32)
            put_from_tiles(stage_gen, j * Q, message, 0)
            put_from_tiles(stage_ham, j * Q, message, TILES)
            if notes is not None:
                notes[pl.ds(row + j * Q, Q), :] = message[SENT - 8 : SENT - 2]
        right[pl.ds(row, GROUP_ROWS), :] = stage_ham[...].astype(BF16)
        right[pl.ds(ROWS + row, GROUP_ROWS), :] = stage_gen[...].astype(BF16)


CHUNK = 192


def scaled_left(rows, row, half, occupancy):
    columns = pl.ds(pl.multiple_of(half * ROWS, LANES), ROWS)
    occ = occupancy[:, columns]
    ham = rows[pl.ds(pl.multiple_of(row, 16), CHUNK), columns].astype(F32) * -occ
    gen = rows[pl.ds(pl.multiple_of(ROWS + row, 16), CHUNK), columns].astype(F32) * occ
    return jnp.concatenate([gen.astype(BF16), ham.astype(BF16)], axis=1)


def own_kernel(ints, occupancy, source, rows, notes, partial, stage_gen, stage_ham):
    unpack_into(source, rows, stage_gen, stage_ham, notes)

    @pl.loop(0, ROWS // CHUNK)
    def _(c):
        left = scaled_left(rows, c * CHUNK, ints[0], occupancy)
        at = pl.ds(pl.multiple_of(c * CHUNK, 16), CHUNK)
        partial[at, :] = jnp.dot(left, rows[...], preferred_element_type=F32)


RESIDENT_LIMIT = 32 * 2**20


def own_half(ints, occupancy, received):
    vmem = pl.BlockSpec(memory_space=pltpu.VMEM)
    return pl.pallas_call(
        own_kernel,
        out_shape=(
            jax.ShapeDtypeStruct((M, M), BF16),
            jax.ShapeDtypeStruct((ROWS, LANES), F32),
            jax.ShapeDtypeStruct((ROWS, M), F32),
        ),
        in_specs=[smem(), vmem, vmem],
        out_specs=(vmem, vmem, vmem),
        scratch_shapes=[pltpu.VMEM((GROUP_ROWS, M), F32), pltpu.VMEM((GROUP_ROWS, M), F32)],
        compiler_params=params(RESIDENT_LIMIT),
        cost_estimate=cost(4 * ROWS * ROWS * M, 16 * ROWS * M),
    )(ints, occupancy, received)


def other_kernel(
    ints, occupancy, source, rows, partial, out, right, stage_gen, stage_ham, product, message
):
    unpack_into(source, right, stage_gen, stage_ham)

    @pl.loop(0, ROWS // CHUNK)
    def _(c):
        left = scaled_left(rows, c * CHUNK, 1 - ints[0], occupancy)
        at = pl.ds(pl.multiple_of(c * CHUNK, 16), CHUNK)
        product[...] = partial[at, :] + jnp.dot(left, right[...], preferred_element_type=F32)
        pairs = CHUNK // Q // 2
        for j in range(pairs):
            put_packed(message.at[j], 0, product, 2 * j * Q)
            put_packed(message.at[j], 8, product, (2 * j + 1) * Q)
            out[c * pairs + j] = message[j].astype(BF16)


def other_half(ints, occupancy, received, rows, partial):
    vmem = pl.BlockSpec(memory_space=pltpu.VMEM)
    return pl.pallas_call(
        other_kernel,
        out_shape=jax.ShapeDtypeStruct((NCH // 2, 16, WIDE), BF16),
        in_specs=[smem(), vmem, vmem, vmem, vmem],
        out_specs=vmem,
        scratch_shapes=[
            pltpu.VMEM((M, M), BF16),
            pltpu.VMEM((GROUP_ROWS, M), F32),
            pltpu.VMEM((GROUP_ROWS, M), F32),
            pltpu.VMEM((CHUNK, M), F32),
            pltpu.VMEM((CHUNK // Q // 2, 16, WIDE), F32),
        ],
        compiler_params=params(RESIDENT_LIMIT),
        cost_estimate=cost(4 * ROWS * ROWS * M, 16 * ROWS * M),
    )(ints, occupancy, received, rows, partial)


def ladder_kernel(
    ints, gen_own, gen_oth, ham_own, ham_oth, occ_own, occ_oth, ham, ham_swapped, gen, gen_swapped, out
):
    def product(left, occ, right, sign):
        scaled = (left[...].astype(F32) * (occ[...] * sign)).astype(BF16)
        return jnp.dot(scaled, right[...], preferred_element_type=F32)

    out[...] = (
        product(gen_own, occ_own, ham, 1.0)
        + product(gen_oth, occ_oth, ham_swapped, 1.0)
        + product(ham_own, occ_own, gen, -1.0)
        + product(ham_oth, occ_oth, gen_swapped, -1.0)
    )


def make_ladder(ints, occupancy, gen, ham):
    def own(i, ints):
        return (i, ints[0])

    def oth(i, ints):
        return (i, 1 - ints[0])

    own_left = pl.BlockSpec((STEP_ROWS, ROWS), own)
    oth_left = pl.BlockSpec((STEP_ROWS, ROWS), oth)
    right = pl.BlockSpec((ROWS, M), lambda i, ints: (0, 0))
    return pl.pallas_call(
        ladder_kernel,
        out_shape=jax.ShapeDtypeStruct((ROWS, M), F32),
        grid_spec=pltpu.PrefetchScalarGridSpec(
            num_scalar_prefetch=1,
            grid=(STEPS,),
            in_specs=[
                own_left,
                oth_left,
                own_left,
                oth_left,
                pl.BlockSpec((1, ROWS), lambda i, ints: (0, ints[0])),
                pl.BlockSpec((1, ROWS), lambda i, ints: (0, 1 - ints[0])),
                right,
                right,
                right,
                right,
            ],
            out_specs=pl.BlockSpec((STEP_ROWS, M), lambda i, ints: (i, 0)),
        ),
        compiler_params=params(),
        cost_estimate=cost(8 * ROWS * ROWS * M, 16 * ROWS * M),
    )(ints, gen, gen, ham, ham, occupancy, occupancy, ham, swap(ham), gen, swap(gen))


def orbit_kernel(ints, degeneracy, notes, own_notes, crossed, ladder, out, stage):
    step = pl.program_id(0)

    @pl.when(step == 0)
    def _():
        out[...] = jnp.zeros_like(out)

    @pl.loop(0, STEP_GROUPS)
    def _(g):
        for j in range(GROUP // 2):
            pair = crossed[g * (GROUP // 2) + j].astype(F32)
            put_unpacked(stage, 2 * j * Q, pair[0:8])
            put_unpacked(stage, (2 * j + 1) * Q, pair[8:16])
        at = pl.ds(pl.multiple_of(g * GROUP_ROWS, 16), GROUP_ROWS)
        first = ints[0] * ROWS + step * STEP_ROWS + g * GROUP_ROWS
        columns = lax.broadcasted_iota(jnp.int32, (GROUP_ROWS, M), 1)
        rows = first + lax.broadcasted_iota(jnp.int32, (GROUP_ROWS, M), 0)
        orbits = lax.broadcasted_iota(jnp.int32, (GROUP_ROWS, 256), 1)
        weight = notes[at, 0:1] + notes[at, 1:2] + notes[at, 2:3]
        place = ints[0] * ROWS + (notes[at, 4:5] * Q + notes[at, 5:6]).astype(jnp.int32)
        own_weight = jnp.where(rows[:, 0:1] < ints[1], degeneracy[0], 0.0)

        def sums(mask, values, weight, orbit):
            picked = jnp.sum(jnp.where(mask, values, 0.0), axis=1, keepdims=True) * weight
            match = orbits == orbit.astype(jnp.int32)
            return jnp.sum(jnp.where(match, picked, 0.0), axis=0, keepdims=True)

        out[...] += sums(columns == place, stage[...], weight, notes[at, 3:4]) + sums(
            columns == rows, ladder[at, :], own_weight, own_notes[at, 3:4]
        )


def orbit_sums(ints, degeneracy, notes, own_notes, crossed, ladder):
    noted = pl.BlockSpec((STEP_ROWS, LANES), lambda i: (i, 0))
    return pl.pallas_call(
        orbit_kernel,
        out_shape=jax.ShapeDtypeStruct((1, 256), F32),
        grid=(STEPS,),
        in_specs=[
            smem(),
            smem(),
            noted,
            noted,
            pl.BlockSpec((STEP_ROWS // Q // 2, 16, WIDE), lambda i: (i, 0, 0)),
            pl.BlockSpec((STEP_ROWS, M), lambda i: (i, 0)),
        ],
        out_specs=pl.BlockSpec((1, 256), lambda i: (0, 0)),
        scratch_shapes=[pltpu.VMEM((GROUP_ROWS, M), F32)],
        compiler_params=params(RESIDENT_LIMIT),
        cost_estimate=cost(10**7, 6 * ROWS * M),
    )(ints, degeneracy, notes, own_notes, crossed, ladder)


def finish_kernel(ints, partner, coupling, back, ladder, out, stage):
    step = pl.program_id(0)

    @pl.loop(0, STEP_GROUPS)
    def _(g):
        group = step * STEP_GROUPS + g
        for j in range(GROUP):
            piece = group * GROUP + j
            source = partner[piece]
            pair = back[source // 2].astype(F32)
            message = jnp.where(source % 2 == 1, pair[8:16], pair[0:8]) * coupling[piece]
            put_unpacked(stage, j * Q, message)
        live = live_block(ints[0], group * GROUP_ROWS, ints[1])
        rows = pl.ds(pl.multiple_of(g * GROUP_ROWS, 16), GROUP_ROWS)
        out[rows, :] = jnp.where(live, ladder[rows, :] + stage[...], 0.0).astype(BF16)


def finish(ints, partner, coupling, back, ladder):
    block = pl.BlockSpec((STEP_ROWS, M), lambda i: (i, 0))
    return pl.pallas_call(
        finish_kernel,
        out_shape=jax.ShapeDtypeStruct((ROWS, M), BF16),
        grid=(STEPS,),
        in_specs=[
            smem(),
            smem(),
            smem(),
            pl.BlockSpec((NCH // 2, 16, WIDE), lambda i: (0, 0, 0)),
            block,
        ],
        out_specs=block,
        scratch_shapes=[pltpu.VMEM((GROUP_ROWS, M), F32)],
        compiler_params=params(),
        cost_estimate=cost(10**7, 8 * ROWS * M),
    )(ints, partner, coupling, back, ladder)


def exchanged(values, axis, size):
    return [
        lax.ppermute(values, axis, [(i, i ^ d) for i in range(size)]) for d in range(1, size)
    ]


def total(values):
    for axis, size in SIZES:
        parts = [values] + exchanged(values, axis, size)
        while len(parts) > 1:
            parts = [parts[i] + parts[i + 1] for i in range(0, len(parts), 2)]
        values = parts[0]
    return values


def swap(array):
    return lax.ppermute(array, "blk", [(0, 1), (1, 0)])


def to_channels(messages):
    return lax.all_to_all(messages, CHAN, split_axis=0, concat_axis=0, tiled=True)


def on_device(
    generator,
    hamiltonian,
    pp_occupancy,
    ph_occupancy,
    lengths,
    partner,
    coupling,
    degeneracy,
    orbital,
):
    blk = lax.axis_index("blk").astype(jnp.int32)
    length = lengths[0]
    ints = jnp.stack([blk, length])
    gen, ham = generator[0], hamiltonian[0]
    sent, own_notes = pack(
        ints, partner[0], coupling[0], degeneracy, orbital.astype(F32), gen, ham
    )
    received = to_channels(sent)

    live_states = jnp.arange(M, dtype=jnp.int32) < length
    occupancy = jnp.where(live_states, pp_occupancy[0], 0.0)[None]
    ladder = make_ladder(ints, occupancy, gen, ham)
    received, ladder = lax.optimization_barrier((received, ladder))

    other = swap(received)
    rows, notes, partial = own_half(ints, ph_occupancy, received)
    crossed = other_half(ints, ph_occupancy, other, rows, partial)
    returned = to_channels(crossed.reshape(NCH, 8, WIDE)).reshape(NCH // 2, 16, WIDE)
    sums = total(orbit_sums(ints, degeneracy, notes, own_notes, crossed, ladder))
    two_body = finish(ints, partner[0], coupling[0], returned, ladder)
    one_body = sums[0, :NOB] / (8.0 * math.sqrt(NCH * M / NOB))
    return (two_body[None], one_body)


def solution(mesh):
    torus = Mesh(
        mesh.devices.reshape(4, 8, 4, mesh.shape["blk"]), ("chan_0", "chan_1", "chan_2", "blk")
    )
    in_specs = (
        P(CHAN, "blk", None),
        P(CHAN, "blk", None),
        P(CHAN, None),
        P(CHAN, None),
        P(CHAN),
        P(CHAN, None),
        P(CHAN, None),
        P(CHAN),
        P(CHAN, "blk"),
    )
    out_specs = (P(CHAN, "blk", None), P())
    return jax.shard_map(
        on_device, mesh=torus, in_specs=in_specs, out_specs=out_specs, check_vma=False
    )
```

```python
import math

import jax
import jax.numpy as jnp
from jax import lax
from jax.experimental import pallas as pl
from jax.experimental.pallas import tpu as pltpu
from jax.sharding import Mesh
from jax.sharding import PartitionSpec as P

NOB = 240
CHAN = ("chan_0", "chan_1", "chan_2")
ROUNDS = (
    ("blk", 2, (1,)),
    ("chan_0", 4, (1, 2, 3)),
    ("chan_2", 4, (1, 2, 3)),
    ("chan_1", 8, (1, 2, 3)),
    ("chan_1", 8, (4,)),
)
M = 1536
ROWS = 768
NCH = 128
Q = 6
WIDE = 1152
TILES = 9
LANES = 128
SENT = 8 * (2 * TILES + 1)
TAIL = 384
GROUP = 8
GROUP_ROWS = GROUP * Q
F32 = jnp.float32
BF16 = jnp.bfloat16


VMEM_LIMIT = 62 * 2**20
STEP_ROWS = 192
STEP_GROUPS = STEP_ROWS // GROUP_ROWS
STEPS = ROWS // STEP_ROWS


def put_packed(dst, at, src, row, scale=None):
    def part(rows, columns):
        block = src[rows, columns]
        return block if scale is None else block * scale

    dst[at : at + Q, :] = part(slice(row, row + Q), slice(0, WIDE))
    for t in range(3):
        dst[at + Q : at + Q + 2, t * TAIL : (t + 1) * TAIL] = part(
            slice(row + 2 * t, row + 2 * t + 2), slice(WIDE, M)
        )


def put_unpacked(dst, row, message):
    dst[row : row + Q, 0:WIDE] = message[0:Q]
    for t in range(3):
        dst[row + 2 * t : row + 2 * t + 2, WIDE:M] = message[Q : Q + 2, t * TAIL : (t + 1) * TAIL]


def params(limit=VMEM_LIMIT):
    return pltpu.CompilerParams(vmem_limit_bytes=limit)


def cost(flops, moved):
    return pl.CostEstimate(flops=flops, bytes_accessed=moved, transcendentals=0)


def smem():
    return pl.BlockSpec(memory_space=pltpu.SMEM)


def put_tiles(dst, tile, src, row, scale):
    for t in range(TILES):
        at = 8 * (tile + t)
        dst[at : at + Q, :] = src[row : row + Q, t * LANES : (t + 1) * LANES] * scale
        pair, third = row + 2 * (t // 3), WIDE + (t % 3) * LANES
        dst[at + Q : at + 8, :] = src[pair : pair + 2, third : third + LANES] * scale


def put_from_tiles(dst, row, message, tile):
    for t in range(TILES):
        at = 8 * (tile + t)
        dst[row : row + Q, t * LANES : (t + 1) * LANES] = message[at : at + Q]
        pair, third = row + 2 * (t // 3), WIDE + (t % 3) * LANES
        dst[pair : pair + 2, third : third + LANES] = message[at + Q : at + 8]


PACK_ROWS = 2 * GROUP_ROWS
PACKS = ROWS // PACK_ROWS
PACK_PIECES = PACK_ROWS // Q
UNROLLED = 4


def note_rows(blk, length, coupling, degeneracy, orbital, notes):
    rows = lax.broadcasted_iota(jnp.int32, (Q, LANES), 0)
    lanes = lax.broadcasted_iota(jnp.int32, (Q, LANES), 1)

    @pl.loop(0, NCH // UNROLLED)
    def _(h):
        some = notes.at[pl.ds(pl.multiple_of(h * UNROLLED * Q, 8), UNROLLED * Q)]
        for j in range(UNROLLED):
            piece = h * UNROLLED + j
            marks = jnp.where(lanes == 4, piece, rows).astype(F32)
            some[j * Q : (j + 1) * Q, :] = jnp.where(
                lanes < 4, coupling[piece] * degeneracy[0], jnp.where(lanes < 6, marks, 0.0)
            )

    @pl.loop(0, ROWS // LANES)
    def _(block):
        at = pl.ds(pl.multiple_of(block * LANES, LANES), LANES)
        here = lax.broadcasted_iota(jnp.int32, (LANES, LANES), 0)
        lanes = lax.broadcasted_iota(jnp.int32, (LANES, LANES), 1)
        orbit = jnp.sum(
            jnp.where(lanes == here, orbital[:, at], 0).astype(F32), axis=1, keepdims=True
        )
        filled = notes[at, :]
        weight = jnp.where(blk * ROWS + block * LANES + here < length, filled, 0.0)
        high = weight.astype(BF16).astype(F32)
        middle = (weight - high).astype(BF16).astype(F32)
        low = weight - high - middle
        noted = jnp.where(lanes == 0, high, jnp.where(lanes == 1, middle, low))
        notes[at, :] = jnp.where(lanes == 3, orbit, jnp.where(lanes < 3, noted, filled))


def pack_kernel(
    lengths,
    partner,
    coupling,
    degeneracy,
    orbital,
    gen,
    ham,
    out,
    notes,
    held_gen,
    held_ham,
    stage_gen,
    stage_ham,
    message,
    ready,
    in_sem,
    sem,
):
    blk, length = lax.axis_index("blk"), lengths[0]

    def fetches(c):
        at = pl.ds(pl.multiple_of(c * PACK_ROWS, 16), PACK_ROWS)
        return (
            pltpu.make_async_copy(gen.at[at], held_gen.at[at], in_sem.at[c, 0]),
            pltpu.make_async_copy(ham.at[at], held_ham.at[at], in_sem.at[c, 1]),
        )

    def copy(piece):
        return pltpu.make_async_copy(ready.at[piece], out.at[partner[piece]], sem.at[0])

    for c in range(PACKS):
        for fetch in fetches(c):
            fetch.start()
    note_rows(blk, length, coupling, degeneracy, orbital, notes)

    @pl.loop(0, PACKS)
    def _(c):
        for fetch in fetches(c):
            fetch.wait()

        @pl.loop(0, PACK_ROWS // 16)
        def _(r):
            at = pl.ds(pl.multiple_of(c * PACK_ROWS + r * 16, 16), 16)
            here = pl.ds(pl.multiple_of(r * 16, 16), 16)
            rows = blk * ROWS + c * PACK_ROWS + r * 16 + lax.broadcasted_iota(jnp.int32, (16, M), 0)
            columns = lax.broadcasted_iota(jnp.int32, (16, M), 1)
            live = (rows < length) & (columns < length)
            stage_gen[here, :] = jnp.where(live, held_gen[at, :].astype(F32), 0.0)
            stage_ham[here, :] = jnp.where(live, held_ham[at, :].astype(F32), 0.0)

        @pl.loop(0, PACK_PIECES // UNROLLED)
        def _(h):
            some = pl.ds(pl.multiple_of(h * UNROLLED * Q, 8), UNROLLED * Q)
            some_gen, some_ham = stage_gen.at[some], stage_ham.at[some]
            some_notes = notes.at[pl.ds(pl.multiple_of(c * PACK_ROWS + h * UNROLLED * Q, 8), UNROLLED * Q)]
            first = c * PACK_PIECES + h * UNROLLED
            for j in range(UNROLLED):
                scale = coupling[first + j]
                put_tiles(message.at[j], 0, some_gen, j * Q, scale)
                put_tiles(message.at[j], TILES, some_ham, j * Q, scale)
                message[j, SENT - 8 : SENT - 2, :] = some_notes[j * Q : (j + 1) * Q, :]
            for j in range(UNROLLED):
                ready[first + j] = message[j].astype(BF16)
                copy(first + j).start()

    pltpu.make_async_copy(ready, out, sem.at[0]).wait()


def pack(lengths, partner, coupling, degeneracy, orbital, generator, hamiltonian):
    vmem = pl.BlockSpec(memory_space=pltpu.VMEM)
    away = pl.BlockSpec(memory_space=pl.ANY)
    return pl.pallas_call(
        pack_kernel,
        out_shape=(
            jax.ShapeDtypeStruct((NCH, SENT, LANES), BF16),
            jax.ShapeDtypeStruct((ROWS, LANES), F32),
        ),
        in_specs=[smem(), smem(), smem(), smem(), vmem, away, away],
        out_specs=(away, vmem),
        scratch_shapes=[
            pltpu.VMEM((ROWS, M), BF16),
            pltpu.VMEM((ROWS, M), BF16),
            pltpu.VMEM((PACK_ROWS, M), F32),
            pltpu.VMEM((PACK_ROWS, M), F32),
            pltpu.VMEM((PACK_PIECES, SENT, LANES), F32),
            pltpu.VMEM((NCH, SENT, LANES), BF16),
            pltpu.SemaphoreType.DMA((PACKS, 2)),
            pltpu.SemaphoreType.DMA((1,)),
        ],
        compiler_params=params(),
        cost_estimate=cost(10**7, 8 * ROWS * M),
    )(lengths, partner, coupling, degeneracy, orbital, generator, hamiltonian)


def unpack_into(source, right, stage_gen, stage_ham, notes=None):
    @pl.loop(0, NCH // GROUP)
    def _(g):
        row = pl.multiple_of(g * GROUP_ROWS, 16)
        for j in range(GROUP):
            message = source[g * GROUP + j].astype(F32)
            put_from_tiles(stage_gen, j * Q, message, 0)
            put_from_tiles(stage_ham, j * Q, message, TILES)
            if notes is not None:
                notes[pl.ds(row + j * Q, Q), :] = message[SENT - 8 : SENT - 2]
        right[pl.ds(row, GROUP_ROWS), :] = stage_ham[...].astype(BF16)
        right[pl.ds(ROWS + row, GROUP_ROWS), :] = stage_gen[...].astype(BF16)


CHUNK = 384
PART = 192


def scaled_left(rows, row, count, half, occupancy):
    columns = pl.ds(pl.multiple_of(half * ROWS, LANES), ROWS)
    occ = occupancy[:, columns]
    ham = rows[pl.ds(pl.multiple_of(row, 16), count), columns].astype(F32) * -occ
    gen = rows[pl.ds(pl.multiple_of(ROWS + row, 16), count), columns].astype(F32) * occ
    return jnp.concatenate([gen.astype(BF16), ham.astype(BF16)], axis=1)


def own_kernel(ints, occupancy, source, rows, notes, partial, stage_gen, stage_ham):
    unpack_into(source, rows, stage_gen, stage_ham, notes)

    @pl.loop(0, ROWS // CHUNK)
    def _(c):
        left = scaled_left(rows, c * CHUNK, CHUNK, ints[0], occupancy)
        at = pl.ds(pl.multiple_of(c * CHUNK, 16), CHUNK)
        partial[at, :] = jnp.dot(left, rows[...], preferred_element_type=F32)


RESIDENT_LIMIT = 32 * 2**20


def own_half(ints, occupancy, received):
    vmem = pl.BlockSpec(memory_space=pltpu.VMEM)
    return pl.pallas_call(
        own_kernel,
        out_shape=(
            jax.ShapeDtypeStruct((M, M), BF16),
            jax.ShapeDtypeStruct((ROWS, LANES), F32),
            jax.ShapeDtypeStruct((ROWS, M), F32),
        ),
        in_specs=[smem(), vmem, vmem],
        out_specs=(vmem, vmem, vmem),
        scratch_shapes=[pltpu.VMEM((GROUP_ROWS, M), F32), pltpu.VMEM((GROUP_ROWS, M), F32)],
        compiler_params=params(RESIDENT_LIMIT),
        cost_estimate=cost(4 * ROWS * ROWS * M, 16 * ROWS * M),
    )(ints, occupancy, received)


def other_kernel(
    ints, occupancy, source, rows, partial, out, right, stage_gen, stage_ham, product, message
):
    unpack_into(source, right, stage_gen, stage_ham)
    pairs = PART // Q // 2
    for c in range(ROWS // PART):
        left = scaled_left(rows, c * PART, PART, 1 - ints[0], occupancy)
        mine = product.at[c % 2]
        mine[...] = partial[c * PART : (c + 1) * PART, :] + jnp.dot(
            left, right[...], preferred_element_type=F32
        )
        for j in range(pairs):
            words = message.at[c % 2, j]
            put_packed(words, 0, mine, 2 * j * Q)
            put_packed(words, 8, mine, (2 * j + 1) * Q)
            out[c * pairs + j] = words[...].astype(BF16)


def other_half(ints, occupancy, received, rows, partial):
    vmem = pl.BlockSpec(memory_space=pltpu.VMEM)
    return pl.pallas_call(
        other_kernel,
        out_shape=jax.ShapeDtypeStruct((NCH // 2, 16, WIDE), BF16),
        in_specs=[smem(), vmem, vmem, vmem, vmem],
        out_specs=vmem,
        scratch_shapes=[
            pltpu.VMEM((M, M), BF16),
            pltpu.VMEM((GROUP_ROWS, M), F32),
            pltpu.VMEM((GROUP_ROWS, M), F32),
            pltpu.VMEM((2, PART, M), F32),
            pltpu.VMEM((2, PART // Q // 2, 16, WIDE), F32),
        ],
        compiler_params=params(RESIDENT_LIMIT),
        cost_estimate=cost(4 * ROWS * ROWS * M, 16 * ROWS * M),
    )(ints, occupancy, received, rows, partial)


def ladder_kernel(
    ints, gen_own, gen_oth, ham_own, ham_oth, occ_own, occ_oth, ham, ham_swapped, gen, gen_swapped, out
):
    def product(left, occ, right, sign):
        scaled = (left[...].astype(F32) * (occ[...] * sign)).astype(BF16)
        return jnp.dot(scaled, right[...], preferred_element_type=F32)

    out[...] = (
        product(gen_own, occ_own, ham, 1.0)
        + product(gen_oth, occ_oth, ham_swapped, 1.0)
        + product(ham_own, occ_own, gen, -1.0)
        + product(ham_oth, occ_oth, gen_swapped, -1.0)
    )


def make_ladder(ints, occupancy, gen, ham):
    def own(i, ints):
        return (i, ints[0])

    def oth(i, ints):
        return (i, 1 - ints[0])

    own_left = pl.BlockSpec((STEP_ROWS, ROWS), own)
    oth_left = pl.BlockSpec((STEP_ROWS, ROWS), oth)
    right = pl.BlockSpec((ROWS, M), lambda i, ints: (0, 0))
    return pl.pallas_call(
        ladder_kernel,
        out_shape=jax.ShapeDtypeStruct((ROWS, M), F32),
        grid_spec=pltpu.PrefetchScalarGridSpec(
            num_scalar_prefetch=1,
            grid=(STEPS,),
            in_specs=[
                own_left,
                oth_left,
                own_left,
                oth_left,
                pl.BlockSpec((1, ROWS), lambda i, ints: (0, ints[0])),
                pl.BlockSpec((1, ROWS), lambda i, ints: (0, 1 - ints[0])),
                right,
                right,
                right,
                right,
            ],
            out_specs=pl.BlockSpec((STEP_ROWS, M), lambda i, ints: (i, 0)),
        ),
        compiler_params=params(),
        cost_estimate=cost(8 * ROWS * ROWS * M, 16 * ROWS * M),
    )(ints, gen, gen, ham, ham, occupancy, occupancy, ham, swap(ham), gen, swap(gen))


def orbit_kernel(ints, degeneracy, notes, own_notes, crossed, ladder, out, stage):
    step = pl.program_id(0)

    @pl.when(step == 0)
    def _():
        out[...] = jnp.zeros_like(out)

    @pl.loop(0, STEP_GROUPS)
    def _(g):
        for j in range(GROUP // 2):
            pair = crossed[g * (GROUP // 2) + j].astype(F32)
            put_unpacked(stage, 2 * j * Q, pair[0:8])
            put_unpacked(stage, (2 * j + 1) * Q, pair[8:16])
        at = pl.ds(pl.multiple_of(g * GROUP_ROWS, 16), GROUP_ROWS)
        first = ints[0] * ROWS + step * STEP_ROWS + g * GROUP_ROWS
        columns = lax.broadcasted_iota(jnp.int32, (GROUP_ROWS, M), 1)
        rows = first + lax.broadcasted_iota(jnp.int32, (GROUP_ROWS, M), 0)
        orbits = lax.broadcasted_iota(jnp.int32, (GROUP_ROWS, 256), 1)
        weight = notes[at, 0:1] + notes[at, 1:2] + notes[at, 2:3]
        place = ints[0] * ROWS + (notes[at, 4:5] * Q + notes[at, 5:6]).astype(jnp.int32)
        own_weight = jnp.where(rows[:, 0:1] < ints[1], degeneracy[0], 0.0)

        def sums(mask, values, weight, orbit):
            picked = jnp.sum(jnp.where(mask, values, 0.0), axis=1, keepdims=True) * weight
            match = orbits == orbit.astype(jnp.int32)
            return jnp.sum(jnp.where(match, picked, 0.0), axis=0, keepdims=True)

        out[...] += sums(columns == place, stage[...], weight, notes[at, 3:4]) + sums(
            columns == rows, ladder[at, :], own_weight, own_notes[at, 3:4]
        )


def orbit_sums(ints, degeneracy, notes, own_notes, crossed, ladder):
    noted = pl.BlockSpec((STEP_ROWS, LANES), lambda i: (i, 0))
    return pl.pallas_call(
        orbit_kernel,
        out_shape=jax.ShapeDtypeStruct((1, 256), F32),
        grid=(STEPS,),
        in_specs=[
            smem(),
            smem(),
            noted,
            noted,
            pl.BlockSpec((STEP_ROWS // Q // 2, 16, WIDE), lambda i: (i, 0, 0)),
            pl.BlockSpec((STEP_ROWS, M), lambda i: (i, 0)),
        ],
        out_specs=pl.BlockSpec((1, 256), lambda i: (0, 0)),
        scratch_shapes=[pltpu.VMEM((GROUP_ROWS, M), F32)],
        compiler_params=params(),
        cost_estimate=cost(10**7, 6 * ROWS * M),
    )(ints, degeneracy, notes, own_notes, crossed, ladder)


def finish_kernel(ints, partner, coupling, back, ladder, out, stage):
    step = pl.program_id(0)

    @pl.loop(0, STEP_ROWS // PACK_ROWS)
    def _(g):
        group = step * (STEP_ROWS // PACK_ROWS) + g
        for j in range(PACK_PIECES):
            piece = group * PACK_PIECES + j
            source = partner[piece]
            pair = back[source // 2].astype(F32)
            message = jnp.where(source % 2 == 1, pair[8:16], pair[0:8]) * coupling[piece]
            put_unpacked(stage, j * Q, message)
        first = ints[0] * ROWS + group * PACK_ROWS
        live = (first + lax.broadcasted_iota(jnp.int32, (PACK_ROWS, M), 0) < ints[1]) & (
            lax.broadcasted_iota(jnp.int32, (PACK_ROWS, M), 1) < ints[1]
        )
        rows = pl.ds(pl.multiple_of(g * PACK_ROWS, 16), PACK_ROWS)
        out[rows, :] = jnp.where(live, ladder[rows, :] + stage[...], 0.0).astype(BF16)


def finish(ints, partner, coupling, back, ladder):
    block = pl.BlockSpec((STEP_ROWS, M), lambda i: (i, 0))
    return pl.pallas_call(
        finish_kernel,
        out_shape=jax.ShapeDtypeStruct((ROWS, M), BF16),
        grid=(STEPS,),
        in_specs=[
            smem(),
            smem(),
            smem(),
            pl.BlockSpec((NCH // 2, 16, WIDE), lambda i: (0, 0, 0)),
            block,
        ],
        out_specs=block,
        scratch_shapes=[pltpu.VMEM((PACK_ROWS, M), F32)],
        compiler_params=params(),
        cost_estimate=cost(10**7, 8 * ROWS * M),
    )(ints, partner, coupling, back, ladder)


def total(values):
    for axis, size, moves in ROUNDS:
        parts = [values] + [
            lax.ppermute(values, axis, [(i, i ^ d) for i in range(size)]) for d in moves
        ]
        while len(parts) > 1:
            parts = [parts[i] + parts[i + 1] for i in range(0, len(parts), 2)]
        values = parts[0]
    return values


def swap(array):
    return lax.ppermute(array, "blk", [(0, 1), (1, 0)])


def to_channels(messages):
    return lax.all_to_all(messages, CHAN, split_axis=0, concat_axis=0, tiled=True)


def on_device(
    generator,
    hamiltonian,
    pp_occupancy,
    ph_occupancy,
    lengths,
    partner,
    coupling,
    degeneracy,
    orbital,
):
    blk = lax.axis_index("blk").astype(jnp.int32)
    length = lengths[0]
    ints = jnp.stack([blk, length])
    gen, ham = generator[0], hamiltonian[0]
    sent, own_notes = pack(
        lengths, partner[0], coupling[0], degeneracy, orbital, gen, ham
    )
    received = to_channels(sent)

    live_states = jnp.arange(M, dtype=jnp.int32) < length
    occupancy = jnp.where(live_states, pp_occupancy[0], 0.0)[None]
    ladder = make_ladder(ints, occupancy, gen, ham)
    received, ladder = lax.optimization_barrier((received, ladder))

    other = swap(received)
    rows, notes, partial = own_half(ints, ph_occupancy, received)
    crossed = other_half(ints, ph_occupancy, other, rows, partial)
    returned = to_channels(crossed.reshape(NCH, 8, WIDE)).reshape(NCH // 2, 16, WIDE)
    sums = total(orbit_sums(ints, degeneracy, notes, own_notes, crossed, ladder))
    two_body = finish(ints, partner[0], coupling[0], returned, ladder)
    one_body = sums[0, :NOB] / (8.0 * math.sqrt(NCH * M / NOB))
    return (two_body[None], one_body)


def solution(mesh):
    torus = Mesh(
        mesh.devices.reshape(4, 8, 4, mesh.shape["blk"]), ("chan_0", "chan_1", "chan_2", "blk")
    )
    in_specs = (
        P(CHAN, "blk", None),
        P(CHAN, "blk", None),
        P(CHAN, None),
        P(CHAN, None),
        P(CHAN),
        P(CHAN, None),
        P(CHAN, None),
        P(CHAN),
        P(CHAN, "blk"),
    )
    out_specs = (P(CHAN, "blk", None), P())
    return jax.shard_map(
        on_device, mesh=torus, in_specs=in_specs, out_specs=out_specs, check_vma=False
    )
```

```python
import math

import jax
import jax.numpy as jnp
from jax import lax
from jax.experimental import pallas as pl
from jax.experimental.pallas import tpu as pltpu
from jax.sharding import Mesh
from jax.sharding import PartitionSpec as P

NOB = 240
CHAN = ("chan_0", "chan_1", "chan_2")
ROUNDS = (
    ("blk", 2, (1,)),
    ("chan_0", 4, (1, 2, 3)),
    ("chan_2", 4, (1, 2, 3)),
    ("chan_1", 8, (1, 2, 3)),
    ("chan_1", 8, (4,)),
)
M = 1536
ROWS = 768
NCH = 128
Q = 6
WIDE = 1152
TILES = 9
LANES = 128
SENT = 8 * (2 * TILES + 1)
TAIL = 384
GROUP = 8
GROUP_ROWS = GROUP * Q
F32 = jnp.float32
BF16 = jnp.bfloat16


VMEM_LIMIT = 62 * 2**20
STEP_ROWS = 192
STEP_GROUPS = STEP_ROWS // GROUP_ROWS
STEPS = ROWS // STEP_ROWS


def put_packed(dst, at, src, row, scale=None):
    def part(rows, columns):
        block = src[rows, columns]
        return block if scale is None else block * scale

    dst[at : at + Q, :] = part(slice(row, row + Q), slice(0, WIDE))
    for t in range(3):
        dst[at + Q : at + Q + 2, t * TAIL : (t + 1) * TAIL] = part(
            slice(row + 2 * t, row + 2 * t + 2), slice(WIDE, M)
        )


def put_unpacked(dst, row, message):
    dst[row : row + Q, 0:WIDE] = message[0:Q]
    for t in range(3):
        dst[row + 2 * t : row + 2 * t + 2, WIDE:M] = message[Q : Q + 2, t * TAIL : (t + 1) * TAIL]


def params(limit=VMEM_LIMIT):
    return pltpu.CompilerParams(vmem_limit_bytes=limit)


def cost(flops, moved):
    return pl.CostEstimate(flops=flops, bytes_accessed=moved, transcendentals=0)


def smem():
    return pl.BlockSpec(memory_space=pltpu.SMEM)


def put_tiles(dst, tile, src, row, scale):
    for t in range(TILES):
        at = 8 * (tile + t)
        dst[at : at + Q, :] = src[row : row + Q, t * LANES : (t + 1) * LANES] * scale
        pair, third = row + 2 * (t // 3), WIDE + (t % 3) * LANES
        dst[at + Q : at + 8, :] = src[pair : pair + 2, third : third + LANES] * scale


def put_from_tiles(dst, row, message, tile):
    for t in range(TILES):
        at = 8 * (tile + t)
        dst[row : row + Q, t * LANES : (t + 1) * LANES] = message[at : at + Q]
        pair, third = row + 2 * (t // 3), WIDE + (t % 3) * LANES
        dst[pair : pair + 2, third : third + LANES] = message[at + Q : at + 8]


PACK_ROWS = 2 * GROUP_ROWS
PACKS = ROWS // PACK_ROWS
PACK_PIECES = PACK_ROWS // Q
UNROLLED = 4


def note_rows(blk, length, coupling, degeneracy, orbital, notes):
    rows = lax.broadcasted_iota(jnp.int32, (Q, LANES), 0)
    lanes = lax.broadcasted_iota(jnp.int32, (Q, LANES), 1)

    @pl.loop(0, NCH // UNROLLED)
    def _(h):
        some = notes.at[pl.ds(pl.multiple_of(h * UNROLLED * Q, 8), UNROLLED * Q)]
        for j in range(UNROLLED):
            piece = h * UNROLLED + j
            marks = jnp.where(lanes == 4, piece, rows).astype(F32)
            some[j * Q : (j + 1) * Q, :] = jnp.where(
                lanes < 4, coupling[piece] * degeneracy[0], jnp.where(lanes < 6, marks, 0.0)
            )

    @pl.loop(0, ROWS // LANES)
    def _(block):
        at = pl.ds(pl.multiple_of(block * LANES, LANES), LANES)
        here = lax.broadcasted_iota(jnp.int32, (LANES, LANES), 0)
        lanes = lax.broadcasted_iota(jnp.int32, (LANES, LANES), 1)
        orbit = jnp.sum(
            jnp.where(lanes == here, orbital[:, at], 0).astype(F32), axis=1, keepdims=True
        )
        filled = notes[at, :]
        weight = jnp.where(blk * ROWS + block * LANES + here < length, filled, 0.0)
        high = weight.astype(BF16).astype(F32)
        middle = (weight - high).astype(BF16).astype(F32)
        low = weight - high - middle
        noted = jnp.where(lanes == 0, high, jnp.where(lanes == 1, middle, low))
        notes[at, :] = jnp.where(lanes == 3, orbit, jnp.where(lanes < 3, noted, filled))


def pack_kernel(
    lengths,
    partner,
    coupling,
    degeneracy,
    orbital,
    gen,
    ham,
    out,
    notes,
    held_gen,
    held_ham,
    stage_gen,
    stage_ham,
    message,
    ready,
    in_sem,
    sem,
):
    blk, length = lax.axis_index("blk"), lengths[0]

    def fetches(c):
        at = pl.ds(pl.multiple_of(c * PACK_ROWS, 16), PACK_ROWS)
        return (
            pltpu.make_async_copy(gen.at[at], held_gen.at[at], in_sem.at[c, 0]),
            pltpu.make_async_copy(ham.at[at], held_ham.at[at], in_sem.at[c, 1]),
        )

    def copy(piece):
        return pltpu.make_async_copy(ready.at[piece], out.at[partner[piece]], sem.at[0])

    for c in range(PACKS):
        for fetch in fetches(c):
            fetch.start()
    note_rows(blk, length, coupling, degeneracy, orbital, notes)

    @pl.loop(0, PACKS)
    def _(c):
        for fetch in fetches(c):
            fetch.wait()

        @pl.loop(0, PACK_ROWS // 16)
        def _(r):
            at = pl.ds(pl.multiple_of(c * PACK_ROWS + r * 16, 16), 16)
            here = pl.ds(pl.multiple_of(r * 16, 16), 16)
            rows = blk * ROWS + c * PACK_ROWS + r * 16 + lax.broadcasted_iota(jnp.int32, (16, M), 0)
            columns = lax.broadcasted_iota(jnp.int32, (16, M), 1)
            live = (rows < length) & (columns < length)
            stage_gen[here, :] = jnp.where(live, held_gen[at, :].astype(F32), 0.0)
            stage_ham[here, :] = jnp.where(live, held_ham[at, :].astype(F32), 0.0)

        @pl.loop(0, PACK_PIECES // UNROLLED)
        def _(h):
            some = pl.ds(pl.multiple_of(h * UNROLLED * Q, 8), UNROLLED * Q)
            some_gen, some_ham = stage_gen.at[some], stage_ham.at[some]
            some_notes = notes.at[pl.ds(pl.multiple_of(c * PACK_ROWS + h * UNROLLED * Q, 8), UNROLLED * Q)]
            first = c * PACK_PIECES + h * UNROLLED
            for j in range(UNROLLED):
                scale = coupling[first + j]
                put_tiles(message.at[j], 0, some_gen, j * Q, scale)
                put_tiles(message.at[j], TILES, some_ham, j * Q, scale)
                message[j, SENT - 8 : SENT - 2, :] = some_notes[j * Q : (j + 1) * Q, :]
            for j in range(UNROLLED):
                ready[first + j] = message[j].astype(BF16)
                copy(first + j).start()

    pltpu.make_async_copy(ready, out, sem.at[0]).wait()


def pack(lengths, partner, coupling, degeneracy, orbital, generator, hamiltonian):
    vmem = pl.BlockSpec(memory_space=pltpu.VMEM)
    away = pl.BlockSpec(memory_space=pl.ANY)
    return pl.pallas_call(
        pack_kernel,
        out_shape=(
            jax.ShapeDtypeStruct((NCH, SENT, LANES), BF16),
            jax.ShapeDtypeStruct((ROWS, LANES), F32),
        ),
        in_specs=[smem(), smem(), smem(), smem(), vmem, away, away],
        out_specs=(away, vmem),
        scratch_shapes=[
            pltpu.VMEM((ROWS, M), BF16),
            pltpu.VMEM((ROWS, M), BF16),
            pltpu.VMEM((PACK_ROWS, M), F32),
            pltpu.VMEM((PACK_ROWS, M), F32),
            pltpu.VMEM((PACK_PIECES, SENT, LANES), F32),
            pltpu.VMEM((NCH, SENT, LANES), BF16),
            pltpu.SemaphoreType.DMA((PACKS, 2)),
            pltpu.SemaphoreType.DMA((1,)),
        ],
        compiler_params=params(),
        cost_estimate=cost(10**7, 8 * ROWS * M),
    )(lengths, partner, coupling, degeneracy, orbital, generator, hamiltonian)


def unpack_into(source, right, stage_gen, stage_ham, notes=None):
    @pl.loop(0, NCH // GROUP)
    def _(g):
        row = pl.multiple_of(g * GROUP_ROWS, 16)
        for j in range(GROUP):
            message = source[g * GROUP + j].astype(F32)
            put_from_tiles(stage_gen, j * Q, message, 0)
            put_from_tiles(stage_ham, j * Q, message, TILES)
            if notes is not None:
                notes[pl.ds(row + j * Q, Q), :] = message[SENT - 8 : SENT - 2]
        right[pl.ds(row, GROUP_ROWS), :] = stage_ham[...].astype(BF16)
        right[pl.ds(ROWS + row, GROUP_ROWS), :] = stage_gen[...].astype(BF16)


CHUNK = 384
PART = 192


def scaled_left(rows, row, count, half, occupancy):
    columns = pl.ds(pl.multiple_of(half * ROWS, LANES), ROWS)
    occ = occupancy[:, columns]
    ham = rows[pl.ds(pl.multiple_of(row, 16), count), columns].astype(F32) * -occ
    gen = rows[pl.ds(pl.multiple_of(ROWS + row, 16), count), columns].astype(F32) * occ
    return jnp.concatenate([gen.astype(BF16), ham.astype(BF16)], axis=1)


def own_kernel(ints, occupancy, source, rows, notes, partial, stage_gen, stage_ham):
    unpack_into(source, rows, stage_gen, stage_ham, notes)

    @pl.loop(0, ROWS // CHUNK)
    def _(c):
        left = scaled_left(rows, c * CHUNK, CHUNK, ints[0], occupancy)
        at = pl.ds(pl.multiple_of(c * CHUNK, 16), CHUNK)
        partial[at, :] = jnp.dot(left, rows[...], preferred_element_type=F32)


RESIDENT_LIMIT = 32 * 2**20


def own_half(ints, occupancy, received):
    vmem = pl.BlockSpec(memory_space=pltpu.VMEM)
    return pl.pallas_call(
        own_kernel,
        out_shape=(
            jax.ShapeDtypeStruct((M, M), BF16),
            jax.ShapeDtypeStruct((ROWS, LANES), F32),
            jax.ShapeDtypeStruct((ROWS, M), F32),
        ),
        in_specs=[smem(), vmem, vmem],
        out_specs=(vmem, vmem, vmem),
        scratch_shapes=[pltpu.VMEM((GROUP_ROWS, M), F32), pltpu.VMEM((GROUP_ROWS, M), F32)],
        compiler_params=params(RESIDENT_LIMIT),
        cost_estimate=cost(4 * ROWS * ROWS * M, 16 * ROWS * M),
    )(ints, occupancy, received)


def other_kernel(
    ints, occupancy, source, rows, partial, out, right, stage_gen, stage_ham, product, message
):
    unpack_into(source, right, stage_gen, stage_ham)
    pairs = PART // Q // 2
    for c in range(ROWS // PART):
        left = scaled_left(rows, c * PART, PART, 1 - ints[0], occupancy)
        mine = product.at[c % 2]
        mine[...] = partial[c * PART : (c + 1) * PART, :] + jnp.dot(
            left, right[...], preferred_element_type=F32
        )
        for j in range(pairs):
            words = message.at[c % 2, j]
            put_packed(words, 0, mine, 2 * j * Q)
            put_packed(words, 8, mine, (2 * j + 1) * Q)
            out[c * pairs + j] = words[...].astype(BF16)


def other_half(ints, occupancy, received, rows, partial):
    vmem = pl.BlockSpec(memory_space=pltpu.VMEM)
    return pl.pallas_call(
        other_kernel,
        out_shape=jax.ShapeDtypeStruct((NCH // 2, 16, WIDE), BF16),
        in_specs=[smem(), vmem, vmem, vmem, vmem],
        out_specs=vmem,
        scratch_shapes=[
            pltpu.VMEM((M, M), BF16),
            pltpu.VMEM((GROUP_ROWS, M), F32),
            pltpu.VMEM((GROUP_ROWS, M), F32),
            pltpu.VMEM((2, PART, M), F32),
            pltpu.VMEM((2, PART // Q // 2, 16, WIDE), F32),
        ],
        compiler_params=params(RESIDENT_LIMIT),
        cost_estimate=cost(4 * ROWS * ROWS * M, 16 * ROWS * M),
    )(ints, occupancy, received, rows, partial)


def ladder_kernel(
    ints, gen_own, gen_oth, ham_own, ham_oth, occ_own, occ_oth, ham, ham_swapped, gen, gen_swapped, out
):
    def product(left, occ, right, sign):
        scaled = (left[...].astype(F32) * (occ[...] * sign)).astype(BF16)
        return jnp.dot(scaled, right[...], preferred_element_type=F32)

    out[...] = (
        product(gen_own, occ_own, ham, 1.0)
        + product(gen_oth, occ_oth, ham_swapped, 1.0)
        + product(ham_own, occ_own, gen, -1.0)
        + product(ham_oth, occ_oth, gen_swapped, -1.0)
    )


def make_ladder(ints, occupancy, gen, ham):
    def own(i, ints):
        return (i, ints[0])

    def oth(i, ints):
        return (i, 1 - ints[0])

    own_left = pl.BlockSpec((STEP_ROWS, ROWS), own)
    oth_left = pl.BlockSpec((STEP_ROWS, ROWS), oth)
    right = pl.BlockSpec((ROWS, M), lambda i, ints: (0, 0))
    return pl.pallas_call(
        ladder_kernel,
        out_shape=jax.ShapeDtypeStruct((ROWS, M), F32),
        grid_spec=pltpu.PrefetchScalarGridSpec(
            num_scalar_prefetch=1,
            grid=(STEPS,),
            in_specs=[
                own_left,
                oth_left,
                own_left,
                oth_left,
                pl.BlockSpec((1, ROWS), lambda i, ints: (0, ints[0])),
                pl.BlockSpec((1, ROWS), lambda i, ints: (0, 1 - ints[0])),
                right,
                right,
                right,
                right,
            ],
            out_specs=pl.BlockSpec((STEP_ROWS, M), lambda i, ints: (i, 0)),
        ),
        compiler_params=params(),
        cost_estimate=cost(8 * ROWS * ROWS * M, 16 * ROWS * M),
    )(ints, gen, gen, ham, ham, occupancy, occupancy, ham, swap(ham), gen, swap(gen))


def orbit_kernel(ints, degeneracy, notes, own_notes, crossed, ladder, out, stage):
    step = pl.program_id(0)

    @pl.when(step == 0)
    def _():
        out[...] = jnp.zeros_like(out)

    @pl.loop(0, STEP_GROUPS)
    def _(g):
        for j in range(GROUP // 2):
            pair = crossed[g * (GROUP // 2) + j].astype(F32)
            put_unpacked(stage, 2 * j * Q, pair[0:8])
            put_unpacked(stage, (2 * j + 1) * Q, pair[8:16])
        at = pl.ds(pl.multiple_of(g * GROUP_ROWS, 16), GROUP_ROWS)
        first = ints[0] * ROWS + step * STEP_ROWS + g * GROUP_ROWS
        columns = lax.broadcasted_iota(jnp.int32, (GROUP_ROWS, M), 1)
        rows = first + lax.broadcasted_iota(jnp.int32, (GROUP_ROWS, M), 0)
        orbits = lax.broadcasted_iota(jnp.int32, (GROUP_ROWS, 256), 1)
        weight = notes[at, 0:1] + notes[at, 1:2] + notes[at, 2:3]
        place = ints[0] * ROWS + (notes[at, 4:5] * Q + notes[at, 5:6]).astype(jnp.int32)
        own_weight = jnp.where(rows[:, 0:1] < ints[1], degeneracy[0], 0.0)

        def sums(mask, values, weight, orbit):
            picked = jnp.sum(jnp.where(mask, values, 0.0), axis=1, keepdims=True) * weight
            match = orbits == orbit.astype(jnp.int32)
            return jnp.sum(jnp.where(match, picked, 0.0), axis=0, keepdims=True)

        out[...] += sums(columns == place, stage[...], weight, notes[at, 3:4]) + sums(
            columns == rows, ladder[at, :], own_weight, own_notes[at, 3:4]
        )


def orbit_sums(ints, degeneracy, notes, own_notes, crossed, ladder):
    noted = pl.BlockSpec((STEP_ROWS, LANES), lambda i: (i, 0))
    return pl.pallas_call(
        orbit_kernel,
        out_shape=jax.ShapeDtypeStruct((1, 256), F32),
        grid=(STEPS,),
        in_specs=[
            smem(),
            smem(),
            noted,
            noted,
            pl.BlockSpec((STEP_ROWS // Q // 2, 16, WIDE), lambda i: (i, 0, 0)),
            pl.BlockSpec((STEP_ROWS, M), lambda i: (i, 0)),
        ],
        out_specs=pl.BlockSpec((1, 256), lambda i: (0, 0)),
        scratch_shapes=[pltpu.VMEM((GROUP_ROWS, M), F32)],
        compiler_params=params(),
        cost_estimate=cost(10**7, 6 * ROWS * M),
    )(ints, degeneracy, notes, own_notes, crossed, ladder)


def finish_kernel(
    ints, partner, coupling, back_away, ladder, out, back, held, ready, stage, back_sem, in_sem, out_sem
):
    def rows_of(g):
        return pl.ds(pl.multiple_of(g * PACK_ROWS, 16), PACK_ROWS)

    def fetch(g):
        return pltpu.make_async_copy(ladder.at[rows_of(g)], held.at[rows_of(g)], in_sem.at[g])

    messages = pltpu.make_async_copy(back_away, back, back_sem.at[0])
    messages.start()
    for g in range(PACKS):
        fetch(g).start()
    messages.wait()

    @pl.loop(0, PACKS)
    def _(g):
        for j in range(PACK_PIECES):
            piece = g * PACK_PIECES + j
            source = partner[piece]
            pair = back[source // 2].astype(F32)
            message = jnp.where(source % 2 == 1, pair[8:16], pair[0:8]) * coupling[piece]
            put_unpacked(stage, j * Q, message)
        fetch(g).wait()
        first = ints[0] * ROWS + g * PACK_ROWS
        live = (first + lax.broadcasted_iota(jnp.int32, (PACK_ROWS, M), 0) < ints[1]) & (
            lax.broadcasted_iota(jnp.int32, (PACK_ROWS, M), 1) < ints[1]
        )
        rows = rows_of(g)
        ready[rows, :] = jnp.where(live, held[rows, :] + stage[...], 0.0).astype(BF16)
        pltpu.make_async_copy(ready.at[rows], out.at[rows], out_sem.at[0]).start()

    pltpu.make_async_copy(ready, out, out_sem.at[0]).wait()


def finish(ints, partner, coupling, back, ladder):
    away = pl.BlockSpec(memory_space=pl.ANY)
    return pl.pallas_call(
        finish_kernel,
        out_shape=jax.ShapeDtypeStruct((ROWS, M), BF16),
        in_specs=[smem(), smem(), smem(), away, away],
        out_specs=away,
        scratch_shapes=[
            pltpu.VMEM((NCH // 2, 16, WIDE), BF16),
            pltpu.VMEM((ROWS, M), F32),
            pltpu.VMEM((ROWS, M), BF16),
            pltpu.VMEM((PACK_ROWS, M), F32),
            pltpu.SemaphoreType.DMA((1,)),
            pltpu.SemaphoreType.DMA((PACKS,)),
            pltpu.SemaphoreType.DMA((1,)),
        ],
        compiler_params=params(),
        cost_estimate=cost(10**7, 8 * ROWS * M),
    )(ints, partner, coupling, back, ladder)


def total(values):
    for axis, size, moves in ROUNDS:
        parts = [values] + [
            lax.ppermute(values, axis, [(i, i ^ d) for i in range(size)]) for d in moves
        ]
        while len(parts) > 1:
            parts = [parts[i] + parts[i + 1] for i in range(0, len(parts), 2)]
        values = parts[0]
    return values


def swap(array):
    return lax.ppermute(array, "blk", [(0, 1), (1, 0)])


def to_channels(messages):
    return lax.all_to_all(messages, CHAN, split_axis=0, concat_axis=0, tiled=True)


def on_device(
    generator,
    hamiltonian,
    pp_occupancy,
    ph_occupancy,
    lengths,
    partner,
    coupling,
    degeneracy,
    orbital,
):
    blk = lax.axis_index("blk").astype(jnp.int32)
    length = lengths[0]
    ints = jnp.stack([blk, length])
    gen, ham = generator[0], hamiltonian[0]
    sent, own_notes = pack(
        lengths, partner[0], coupling[0], degeneracy, orbital, gen, ham
    )
    received = to_channels(sent)

    live_states = jnp.arange(M, dtype=jnp.int32) < length
    occupancy = jnp.where(live_states, pp_occupancy[0], 0.0)[None]
    ladder = make_ladder(ints, occupancy, gen, ham)
    received, ladder = lax.optimization_barrier((received, ladder))

    other = swap(received)
    rows, notes, partial = own_half(ints, ph_occupancy, received)
    crossed = other_half(ints, ph_occupancy, other, rows, partial)
    returned = to_channels(crossed.reshape(NCH, 8, WIDE)).reshape(NCH // 2, 16, WIDE)
    sums = total(orbit_sums(ints, degeneracy, notes, own_notes, crossed, ladder))
    two_body = finish(ints, partner[0], coupling[0], returned, ladder)
    one_body = sums[0, :NOB] / (8.0 * math.sqrt(NCH * M / NOB))
    return (two_body[None], one_body)


def solution(mesh):
    torus = Mesh(
        mesh.devices.reshape(4, 8, 4, mesh.shape["blk"]), ("chan_0", "chan_1", "chan_2", "blk")
    )
    in_specs = (
        P(CHAN, "blk", None),
        P(CHAN, "blk", None),
        P(CHAN, None),
        P(CHAN, None),
        P(CHAN),
        P(CHAN, None),
        P(CHAN, None),
        P(CHAN),
        P(CHAN, "blk"),
    )
    out_specs = (P(CHAN, "blk", None), P())
    return jax.shard_map(
        on_device, mesh=torus, in_specs=in_specs, out_specs=out_specs, check_vma=False
    )
```
